512 devices in a mesh: dp: 256 (over z, y, x), ctx: 2 (over core).
Axes of the slice: x: 4, y: 8, z: 8, core: 2. Of those that a mesh axis runs over, the one named last changes fastest.
Arguments:
- query_rows: bfloat16 [65536, 1024], P(('dp', 'ctx')), may hold values from -6 to 6
- key_rows: bfloat16 [65536, 1024], P(('dp', 'ctx')), may hold values from -6 to 6
- value_rows: bfloat16 [65536, 1024], P(('dp', 'ctx')), may hold values from -6 to 6
- gate_rows: bfloat16 [65536, 1024], P(('dp', 'ctx')), may hold values from -6 to 6
- lengths: int32 [256, 4], P('dp'), may hold values from 1 to 128, 256 in all within a row
- norm_gain: float32 [1024], replicated, may hold values from 0.3 to 3
- out_weight: bfloat16 [1024, 1024], replicated, may hold values from -0.1875 to 0.1875
- cotangent: bfloat16 [65536, 1024], P(('dp', 'ctx')), may hold values from -6 to 6
Outputs:
- layer_out: bfloat16 [65536, 1024], P(('dp', 'ctx'))
- query_grad: bfloat16 [65536, 1024], P(('dp', 'ctx'))
- key_grad: bfloat16 [65536, 1024], P(('dp', 'ctx'))
- value_grad: bfloat16 [65536, 1024], P(('dp', 'ctx'))
- gate_grad: bfloat16 [65536, 1024], P(('dp', 'ctx'))
- gain_grad: float32 [1024], replicated
- weight_grad: float32 [1024, 1024], replicated
The draws below stay inside these ranges and needn't reach their ends.
Inputs may be any that keep to these rules, and one draw needn't show every extreme that they name: Each row holds the lengths of the 4 users of one packed sequence, in order; they sum to 256, and the largest of each row is 128.
All inputs are finite; a program needn't handle non-finite values.
Results may differ from the reference program's by a relative error of at most 0.0059.
Values may be sent and summed in bfloat16 or wider, within the bound.
No kernel may reach another device: no remote copies, remote signals or barrier semaphores. Data moves between devices by JAX's collectives and lax.ppermute only.
A program may use at most 64 MiB of HBM per device.

```python
import math
import jax
import jax.numpy as jnp
import numpy as np
from jax import lax

HEADS = 4
HEAD_DIM = 256
D = 1024
USERS = 4
GROUP_ROWS = 256
LONGEST = 128
GROUPS = 256
TOKENS = 65536


def level_of(rng, dims, split, smallest, top_value):
    def one(axis_at, blocks):
        draws = jax.random.uniform(jax.random.fold_in(jax.random.fold_in(rng, 6), axis_at), (blocks,), jnp.float32, smallest / len(split), top_value / len(split))
        return jnp.repeat(jnp.exp(draws), dims[axis_at] // blocks).reshape((-1,) + (1,) * (len(dims) - axis_at - 1))

    level = one(*split[0])
    for cut in split[1:]:
        level = level * one(*cut)
    return level


def length_profile(count, total, limit, skew):
    weights = [(1 << 20) // math.isqrt(rank ** skew) + 1 for rank in range(2, count + 1)]
    spare, holding = total - limit - (count - 1), [1] * (count - 1)
    while spare > 0:
        movable = [i for i in range(count - 1) if holding[i] < limit]
        mass, budget = sum([weights[i] for i in movable]), spare
        for i in movable:
            more = min(limit - holding[i], max(1, budget * weights[i] // mass), spare)
            holding[i] = holding[i] + more
            spare = spare - more
    return np.array([limit] + holding)


def uneven_parts(rng, count, total, bound, lean):
    if count == 2:
        one = jax.random.randint(rng, (), max(1, total - bound), min(bound, total - 1) + 1)
        return jnp.stack([one, total - one])
    sizes = jnp.asarray(length_profile(count, total, bound, lean), jnp.int32)
    pairs = (count - 1) // 2
    donor, receiver = sizes[1:1 + 2 * pairs:2], sizes[2:2 + 2 * pairs:2]
    margin = jnp.minimum(donor - 1, bound - receiver)
    passed = jax.random.randint(jax.random.fold_in(rng, 1), (pairs,), 0, 1 << 20) % (margin + 1)
    sizes = sizes.at[1:1 + 2 * pairs:2].set(donor - passed).at[2:2 + 2 * pairs:2].set(receiver + passed)
    return sizes[jax.random.permutation(jax.random.fold_in(rng, 2), count)]


def bell_draw(key, dims, deviation, reach, pieces=(), kind=jnp.bfloat16):
    level = level_of(key, dims, pieces, -0.22, 0.18) if pieces else 1.0
    result = jax.random.normal(key, dims, jnp.float32) * deviation * level
    return jnp.minimum(jnp.maximum(result, -reach), reach).astype(kind)


def setup_inputs(seed: int = 0) -> dict:
    keys = jax.random.split(jax.random.key(seed), 9)
    query_rows = bell_draw(keys[0], (TOKENS, D), 1.0, 6.0, ((0, 512),))
    key_rows = bell_draw(keys[1], (TOKENS, D), 1.0, 6.0, ((0, 512),))
    value_rows = bell_draw(keys[2], (TOKENS, D), 1.0, 6.0, ((0, 512),))
    gate_rows = bell_draw(keys[3], (TOKENS, D), 1.0, 6.0, ((0, 512),))
    lengths = jax.vmap(lambda own: uneven_parts(own, USERS, GROUP_ROWS, LONGEST, 2))(jax.random.split(keys[4], GROUPS)).reshape((GROUPS, USERS)).astype(jnp.int32)
    norm_gain = jnp.clip(jnp.exp(jax.random.uniform(keys[5], (D,), jnp.float32, math.log(0.3), math.log(3.0))), 0.3, 3.0)
    out_weight = bell_draw(keys[6], (D, D), D ** -0.5, 0.1875)
    cotangent = bell_draw(keys[7], (TOKENS, D), 1.0, 6.0, ((0, 512),))
    return dict(query_rows=query_rows, key_rows=key_rows, value_rows=value_rows, gate_rows=gate_rows, lengths=lengths, norm_gain=norm_gain, out_weight=out_weight, cotangent=cotangent)


def user_index(user_ends, positions):
    return lax.optimization_barrier(jnp.sum((positions[:, None] >= user_ends[None, :]).astype(jnp.int32), axis=1, dtype=jnp.int32))

def silu_slope(scores):
    sigma = jax.nn.sigmoid(scores)
    return sigma * (1.0 + scores * (1.0 - sigma))

def reference(query_rows, key_rows, value_rows, gate_rows, lengths, norm_gain, out_weight, cotangent):
    group_len = GROUP_ROWS
    score_scale = HEAD_DIM ** (-0.5)

    def regroup(array):
        return array.reshape(GROUPS, group_len, D)
    stacked = (regroup(query_rows), regroup(key_rows), regroup(value_rows), regroup(gate_rows), regroup(cotangent), lengths)

    def heads_of(array):
        return array.astype(jnp.float32).reshape(group_len, HEADS, HEAD_DIM)

    def per_group(sums, inputs):
        q_in, k_in, v_in, u_in, cot_in, lens_in = inputs
        positions = jnp.arange(group_len, dtype=jnp.int32)
        owners = user_index(jnp.cumsum(lens_in.astype(jnp.int32)).astype(jnp.int32), positions)
        visible = (owners[:, None] == owners[None, :]) & (positions[None, :] <= positions[:, None])
        q_heads = heads_of(q_in)
        k_heads = heads_of(k_in)
        v_heads = heads_of(v_in)
        scores = jnp.einsum('qhd,khd->hqk', q_heads, k_heads) * score_scale
        weights = jnp.where(visible[None], jax.nn.silu(scores), 0.0).astype(jnp.bfloat16)
        weights_wide = lax.optimization_barrier(weights).astype(jnp.float32)
        attended = jnp.einsum('hqk,khd->qhd', weights_wide, v_heads).reshape(group_len, D)
        row_mean = lax.optimization_barrier(jnp.mean(attended, axis=1, keepdims=True))
        centered = attended - row_mean
        row_var = lax.optimization_barrier(jnp.mean(centered * centered, axis=1, keepdims=True))
        inv_std = lax.rsqrt(row_var + 1e-05)
        normed = centered * inv_std
        gate_wide = u_in.astype(jnp.float32)
        gated = (normed * norm_gain * gate_wide).astype(jnp.bfloat16)
        layer_part = jnp.dot(gated, out_weight, preferred_element_type=jnp.float32).astype(jnp.bfloat16)
        gated_grad = jnp.dot(cot_in, out_weight.T, preferred_element_type=jnp.float32)
        weight_part = jnp.dot(gated.T, cot_in, preferred_element_type=jnp.float32)
        gain_part = lax.optimization_barrier(jnp.sum(gated_grad * gate_wide * normed, axis=0))
        gate_part = (gated_grad * normed * norm_gain).astype(jnp.bfloat16)
        inner = gated_grad * gate_wide * norm_gain
        out_grad = ((inner - lax.optimization_barrier(jnp.mean(inner, axis=1, keepdims=True)) - normed * lax.optimization_barrier(jnp.mean(inner * normed, axis=1, keepdims=True))) * inv_std).astype(jnp.bfloat16)
        grad_heads = heads_of(lax.optimization_barrier(out_grad))
        attn_grad = jnp.einsum('qhd,khd->hqk', grad_heads, v_heads)
        score_grad = jnp.where(visible[None], attn_grad * silu_slope(scores), 0.0).astype(jnp.bfloat16)
        score_wide = lax.optimization_barrier(score_grad).astype(jnp.float32)
        query_part = (jnp.einsum('hqk,khd->qhd', score_wide, k_heads) * score_scale).reshape(group_len, D).astype(jnp.bfloat16)
        key_part = (jnp.einsum('hqk,qhd->khd', score_wide, q_heads) * score_scale).reshape(group_len, D).astype(jnp.bfloat16)
        value_part = jnp.einsum('hqk,qhd->khd', weights_wide, grad_heads).reshape(group_len, D).astype(jnp.bfloat16)
        weight_sum, gain_sum = sums
        return ((weight_sum + weight_part, gain_sum + gain_part), (layer_part, query_part, key_part, value_part, gate_part))
    start_sums = (jnp.zeros((D, D), jnp.float32), jnp.zeros((D,), jnp.float32))
    (weight_grad, gain_grad), results = lax.scan(per_group, start_sums, stacked)
    layer_out, query_grad, key_grad, value_grad, gate_grad = [item.reshape(TOKENS, D) for item in results]
    return (layer_out, query_grad, key_grad, value_grad, gate_grad, gain_grad, weight_grad)
```

```python
import functools

import jax
import jax.numpy as jnp
from jax import lax
from jax.experimental import pallas as pl
from jax.experimental.pallas import tpu as pltpu
from jax.sharding import Mesh, PartitionSpec as P

HEADS = 4
HEAD_DIM = 256
WIDTH = 1024
ROWS = 128
GROUP = 256
PLANE = ("z", "y")
CHIPS = ("z", "y", "x")
DEVICES = ("z", "y", "x", "c")
F32 = jnp.float32
BF16 = jnp.bfloat16
VMEM = pl.BlockSpec(memory_space=pltpu.VMEM)
SMEM = pl.BlockSpec(memory_space=pltpu.SMEM)
PARAMS = pltpu.CompilerParams(vmem_limit_bytes=48 * 1024 * 1024)


def dot(a, b, contract):
    return lax.dot_general(a, b, (contract, ((), ())), preferred_element_type=F32)


def visible_mask(core, lengths):
    def place(shape, axis):
        local = lax.broadcasted_iota(jnp.int32, shape, axis)
        return jnp.where(local < ROWS, core * ROWS + local, (1 - core) * ROWS + local - ROWS)

    row, column = place((GROUP, 1), 0), place((GROUP, GROUP), 1)
    start = jnp.zeros((GROUP, 1), jnp.int32)
    end = 0
    for user in range(3):
        end = end + lengths[0, user]
        start = jnp.where(row >= end, end, start)
    return (column <= row) & (column >= start)


def both(own, other, item, columns):
    rows = slice(item * ROWS, (item + 1) * ROWS)
    return jnp.concatenate([own[rows, columns], other[rows, columns]], axis=0)


def head_columns(head):
    return slice(head * HEAD_DIM, (head + 1) * HEAD_DIM)


def forward_kernel(core_ref, lengths, own, other, gain, part, normed, inv_std, gated_own, attended, gated):
    core = core_ref[0]
    visible = visible_mask(core, lengths)
    for head in range(HEADS):
        columns = head_columns(head)
        scores = dot(both(own, other, 0, columns), both(own, other, 1, columns), ((1,), (1,))) * (HEAD_DIM**-0.5)
        weights = jnp.where(visible, scores * jax.nn.sigmoid(scores), 0.0).astype(BF16)
        attended[:, columns] = dot(weights, both(own, other, 2, columns), ((1,), (0,)))
    chunk = 32
    for first in range(0, GROUP, chunk):
        rows = slice(first, first + chunk)
        values = attended[rows, :]
        centered = values - jnp.mean(values, axis=1, keepdims=True)
        inverse = lax.rsqrt(jnp.mean(centered * centered, axis=1, keepdims=True) + 1e-05)
        unit = centered * inverse
        normed[rows, :] = unit
        inv_std[rows, :] = inverse
        source, at = (own, first) if first < ROWS else (other, first - ROWS)
        gate = source[3 * ROWS + at : 3 * ROWS + at + chunk, :].astype(F32)
        result = (unit * gain[...] * gate).astype(BF16)
        gated[0, rows, :] = result[:, : WIDTH // 2]
        gated[1, rows, :] = result[:, WIDTH // 2 :]
        if first < ROWS:
            gated_own[rows, :] = result
    for x in range(4):
        mine = gated[core, :, x * 128 : (x + 1) * 128]
        for half in range(2):
            wide = slice(half * 512, (half + 1) * 512)
            block = dot(mine, both(own, other, 4, wide), ((0,), (0,))).astype(BF16)
            for i in range(8):
                for j in range(4):
                    part[x, i * 8 + half * 4 + j] = block[i * 16 : (i + 1) * 16, j * 128 : (j + 1) * 128]


def backward_kernel(
    core_ref, lengths, own, other, gain, normed, inv_std, gated_own, weight,
    layer_out, query_grad, key_grad, value_grad, gate_grad, gated_grad, out_grad,
):
    core = core_ref[0]
    visible = visible_mask(core, lengths)
    scale = HEAD_DIM**-0.5
    gated_grad[...] = dot(both(own, other, 4, slice(None)), weight[...], ((1,), (1,)))
    layer_out[...] = dot(gated_own[...], weight[...], ((1,), (0,))).astype(BF16)
    chunk = 32
    for first in range(0, GROUP, chunk):
        rows = slice(first, first + chunk)
        unit = normed[rows, :]
        source, at = (own, first) if first < ROWS else (other, first - ROWS)
        gate = source[3 * ROWS + at : 3 * ROWS + at + chunk, :].astype(F32)
        scaled = gated_grad[rows, :] * gain[...]
        if first < ROWS:
            gate_grad[rows, :] = (scaled * unit).astype(BF16)
        inner = scaled * gate
        inner = (
            inner
            - jnp.mean(inner, axis=1, keepdims=True)
            - unit * jnp.mean(inner * unit, axis=1, keepdims=True)
        ) * inv_std[rows, :]
        out_grad[rows, :] = inner.astype(BF16)
    for head in range(HEADS):
        columns = head_columns(head)
        queries, keys = both(own, other, 0, columns), both(own, other, 1, columns)
        values, grads = both(own, other, 2, columns), out_grad[:, columns]
        scores = dot(queries, keys, ((1,), (1,))) * scale
        sigma = jax.nn.sigmoid(scores)
        weights = jnp.where(visible, scores * sigma, 0.0).astype(BF16)
        slope = sigma * (1.0 + scores * (1.0 - sigma))
        score_grad = jnp.where(visible, dot(grads, values, ((1,), (1,))) * slope, 0.0).astype(BF16)
        query_grad[:, columns] = (dot(score_grad[:ROWS, :], keys, ((1,), (0,))) * scale).astype(BF16)
        key_grad[:, columns] = (dot(score_grad[:, :ROWS], queries, ((0,), (0,))) * scale).astype(BF16)
        value_grad[:, columns] = dot(weights[:, :ROWS], grads, ((0,), (0,))).astype(BF16)


def finish_kernel(core_ref, mine, other, weight, gain, weight_grad, gain_grad):
    def write(source):
        total = jnp.zeros((ROWS, 128), F32)
        for j in range(8):
            columns = slice(j * 128, (j + 1) * 128)
            block = jnp.concatenate([source[0, i * 8 + j].astype(F32) for i in range(8)], axis=0)
            weight_grad[:, columns] = block
            total = total + block * weight[:, columns].astype(F32)
        gain_grad[...] = jnp.sum(total.T, axis=0, keepdims=True) / gain[...]

    step = pl.program_id(0)

    @pl.when(step < 4)
    def _():
        write(mine)

    @pl.when(step >= 4)
    def _():
        write(other)


def per_device(query_rows, key_rows, value_rows, gate_rows, lengths, norm_gain, out_weight, cotangent):
    core = lax.axis_index("c").astype(jnp.int32).reshape(1)
    gain = norm_gain.reshape(1, WIDTH)
    swap = [(0, 1), (1, 0)]
    own = jnp.concatenate([query_rows, key_rows, value_rows, gate_rows, cotangent], axis=0)
    other = lax.ppermute(own, "c", swap)
    shape = jax.ShapeDtypeStruct
    part, normed, inv_std, gated_own = pl.pallas_call(
        forward_kernel,
        out_shape=[
            shape((4, 64, 16, 128), BF16),
            shape((GROUP, WIDTH), F32),
            shape((GROUP, 1), F32),
            shape((ROWS, WIDTH), BF16),
        ],
        in_specs=[SMEM, SMEM, VMEM, VMEM, VMEM],
        out_specs=[VMEM] * 4,
        scratch_shapes=[pltpu.VMEM((GROUP, WIDTH), F32), pltpu.VMEM((2, GROUP, WIDTH // 2), BF16)],
        compiler_params=PARAMS,
        cost_estimate=pl.CostEstimate(flops=540_000_000, bytes_accessed=6_000_000, transcendentals=300_000),
        name="forward",
    )(core, lengths, own, other, gain)

    pieces = lax.all_to_all(part, "x", 0, 0, tiled=True)

    layer_out, query_grad, key_grad, value_grad, gate_grad = pl.pallas_call(
        backward_kernel,
        out_shape=[shape((ROWS, WIDTH), BF16)] * 5,
        in_specs=[SMEM, SMEM] + [VMEM] * 7,
        out_specs=[VMEM] * 5,
        scratch_shapes=[pltpu.VMEM((GROUP, WIDTH), F32), pltpu.VMEM((GROUP, WIDTH), BF16)],
        compiler_params=PARAMS,
        cost_estimate=pl.CostEstimate(flops=1_800_000_000, bytes_accessed=9_000_000, transcendentals=300_000),
        name="backward",
    )(core, lengths, own, other, gain, normed, inv_std, gated_own, out_weight)

    block = jnp.sum(pieces.astype(F32), axis=0).astype(BF16)
    pieces = lax.all_to_all(block, PLANE, 0, 0, tiled=True)
    total = jnp.sum(pieces.astype(F32), axis=0).astype(BF16)
    block = lax.all_to_all(jnp.broadcast_to(total[None], (64, 16, 128)), PLANE, 0, 0, tiled=True)
    mine = lax.all_to_all(jnp.broadcast_to(block[None], (4, 64, 16, 128)), "x", 0, 0, tiled=True)
    theirs = lax.ppermute(mine, "c", swap)

    def target(step, core):
        return jnp.where(step < 4, core[0], 1 - core[0]) * 4 + step % 4

    weight_grad, gain_grad = pl.pallas_call(
        finish_kernel,
        out_shape=[shape((WIDTH, WIDTH), F32), shape((1, WIDTH), F32)],
        grid_spec=pltpu.PrefetchScalarGridSpec(
            num_scalar_prefetch=1,
            grid=(8,),
            in_specs=[
                pl.BlockSpec((1, 64, 16, 128), lambda s, core: (jnp.minimum(s, 3), 0, 0, 0)),
                pl.BlockSpec((1, 64, 16, 128), lambda s, core: (jnp.maximum(s - 4, 0), 0, 0, 0)),
                pl.BlockSpec((ROWS, WIDTH), lambda s, core: (target(s, core), 0)),
                pl.BlockSpec((1, 128), lambda s, core: (0, target(s, core))),
            ],
            out_specs=[
                pl.BlockSpec((ROWS, WIDTH), lambda s, core: (target(s, core), 0)),
                pl.BlockSpec((1, 128), lambda s, core: (0, target(s, core))),
            ],
        ),
        compiler_params=PARAMS,
        cost_estimate=pl.CostEstimate(flops=3_000_000, bytes_accessed=8_000_000, transcendentals=0),
        name="finish",
    )(core, mine, theirs, out_weight, gain)
    return (layer_out, query_grad, key_grad, value_grad, gate_grad, gain_grad.reshape(WIDTH), weight_grad)


def solution(mesh):
    chips = Mesh(mesh.devices.reshape(8, 8, 4, 2), DEVICES)
    rows = P(DEVICES, None)
    return jax.shard_map(
        per_device,
        mesh=chips,
        in_specs=(rows, rows, rows, rows, P(CHIPS, None), P(), P(), rows),
        out_specs=(rows, rows, rows, rows, rows, P(), P()),
        check_vma=False,
    )
```

```python
import functools

import jax
import jax.numpy as jnp
from jax import lax
from jax.experimental import pallas as pl
from jax.experimental.pallas import tpu as pltpu
from jax.sharding import Mesh, PartitionSpec as P

HEADS = 4
HEAD_DIM = 256
WIDTH = 1024
ROWS = 128
GROUP = 256
PLANE = ("z", "y")
CHIPS = ("z", "y", "x")
DEVICES = ("z", "y", "x", "c")
F32 = jnp.float32
BF16 = jnp.bfloat16
VMEM = pl.BlockSpec(memory_space=pltpu.VMEM)
SMEM = pl.BlockSpec(memory_space=pltpu.SMEM)
PARAMS = pltpu.CompilerParams(vmem_limit_bytes=20 * 1024 * 1024)


def dot(a, b, contract):
    return lax.dot_general(a, b, (contract, ((), ())), preferred_element_type=F32)


def visible_mask(core, lengths):
    def place(shape, axis):
        local = lax.broadcasted_iota(jnp.int32, shape, axis)
        return jnp.where(local < ROWS, core * ROWS + local, (1 - core) * ROWS + local - ROWS)

    row, column = place((GROUP, 1), 0), place((GROUP, GROUP), 1)
    start = jnp.zeros((GROUP, 1), jnp.int32)
    end = 0
    for user in range(3):
        end = end + lengths[0, user]
        start = jnp.where(row >= end, end, start)
    return (column <= row) & (column >= start)


def both(own, other, item, columns):
    rows = slice(item * ROWS, (item + 1) * ROWS)
    return jnp.concatenate([own[rows, columns], other[rows, columns]], axis=0)


def head_columns(head):
    return slice(head * HEAD_DIM, (head + 1) * HEAD_DIM)


def tile(index):
    return slice(index * 16, (index + 1) * 16)


def forward_kernel(lengths, own, other, gain, part, normed, inv_std, gated_own, attended, gated):
    core = lax.axis_index("c")
    visible = visible_mask(core, lengths)
    for head in range(HEADS):
        columns = head_columns(head)
        scores = dot(both(own, other, 0, columns), both(own, other, 1, columns), ((1,), (1,))) * (HEAD_DIM**-0.5)
        weights = jnp.where(visible, scores * jax.nn.sigmoid(scores), 0.0).astype(BF16)
        attended[:, columns] = dot(weights, both(own, other, 2, columns), ((1,), (0,)))
    chunk = 32
    for first in range(0, GROUP, chunk):
        rows = slice(first, first + chunk)
        values = attended[rows, :]
        centered = values - jnp.mean(values, axis=1, keepdims=True)
        inverse = lax.rsqrt(jnp.mean(centered * centered, axis=1, keepdims=True) + 1e-05)
        unit = centered * inverse
        normed[rows, :] = unit
        inv_std[rows, :] = inverse
        source, at = (own, first) if first < ROWS else (other, first - ROWS)
        gate = source[3 * ROWS + at : 3 * ROWS + at + chunk, :].astype(F32)
        result = (unit * gain[...] * gate).astype(BF16)
        gated[0, rows, :] = result[:, : WIDTH // 2]
        gated[1, rows, :] = result[:, WIDTH // 2 :]
        if first < ROWS:
            gated_own[rows, :] = result
    for x in range(4):
        mine = gated[core, :, x * 128 : (x + 1) * 128]
        for half in range(2):
            wide = slice(half * 512, (half + 1) * 512)
            block = dot(mine, both(own, other, 4, wide), ((0,), (0,))).astype(BF16)
            for i in range(8):
                for j in range(4):
                    part[x, tile(i * 8 + half * 4 + j), :] = block[i * 16 : (i + 1) * 16, j * 128 : (j + 1) * 128]


def backward_kernel(
    lengths, own, other, gain, normed, inv_std, gated_own, weight,
    layer_out, query_grad, key_grad, value_grad, gate_grad, gated_grad, out_grad,
):
    core = lax.axis_index("c")
    visible = visible_mask(core, lengths)
    scale = HEAD_DIM**-0.5
    gated_grad[...] = dot(both(own, other, 4, slice(None)), weight[...], ((1,), (1,)))
    layer_out[...] = dot(gated_own[...], weight[...], ((1,), (0,))).astype(BF16)
    chunk = 32
    for first in range(0, GROUP, chunk):
        rows = slice(first, first + chunk)
        unit = normed[rows, :]
        source, at = (own, first) if first < ROWS else (other, first - ROWS)
        gate = source[3 * ROWS + at : 3 * ROWS + at + chunk, :].astype(F32)
        scaled = gated_grad[rows, :] * gain[...]
        if first < ROWS:
            gate_grad[rows, :] = (scaled * unit).astype(BF16)
        inner = scaled * gate
        inner = (
            inner
            - jnp.mean(inner, axis=1, keepdims=True)
            - unit * jnp.mean(inner * unit, axis=1, keepdims=True)
        ) * inv_std[rows, :]
        out_grad[rows, :] = inner.astype(BF16)
    for head in range(HEADS):
        columns = head_columns(head)
        queries, keys = both(own, other, 0, columns), both(own, other, 1, columns)
        values, grads = both(own, other, 2, columns), out_grad[:, columns]
        scores = dot(queries, keys, ((1,), (1,))) * scale
        sigma = jax.nn.sigmoid(scores)
        weights = jnp.where(visible, scores * sigma, 0.0).astype(BF16)
        slope = sigma * (1.0 + scores * (1.0 - sigma))
        score_grad = jnp.where(visible, dot(grads, values, ((1,), (1,))) * slope, 0.0).astype(BF16)
        query_grad[:, columns] = (dot(score_grad[:ROWS, :], keys, ((1,), (0,))) * scale).astype(BF16)
        key_grad[:, columns] = (dot(score_grad[:, :ROWS], queries, ((0,), (0,))) * scale).astype(BF16)
        value_grad[:, columns] = dot(weights[:, :ROWS], grads, ((0,), (0,))).astype(BF16)


def chip_sum_kernel(pieces, total):
    for first in range(0, 1024, 128):
        rows = slice(first, first + 128)
        value = pieces[0, rows, :].astype(F32) + pieces[1, rows, :].astype(F32)
        total[rows, :] = (value + (pieces[2, rows, :].astype(F32) + pieces[3, rows, :].astype(F32))).astype(BF16)


def plane_sum_kernel(pieces, total):
    sums = [pieces[i].astype(F32) for i in range(4)]
    for first in range(4, 64, 4):
        sums = [sums[i] + pieces[first + i].astype(F32) for i in range(4)]
    value = ((sums[0] + sums[1]) + (sums[2] + sums[3])).astype(BF16)
    for i in range(64):
        total[i] = value


def finish_kernel(source, weight, gain, *rest):
    weight_grad, gain_grad = rest[-2:]
    total = jnp.zeros((ROWS, 128), F32)
    for j in range(8):
        columns = slice(j * 128, (j + 1) * 128)
        block = jnp.concatenate([source[0, tile(i * 8 + j), :].astype(F32) for i in range(8)], axis=0)
        weight_grad[:, columns] = block
        total = total + block * weight[:, columns].astype(F32)
    gain_grad[...] = jnp.sum(total.T, axis=0, keepdims=True) / gain[...]


def finish(theirs, source, weight, gain, partial):
    shape = jax.ShapeDtypeStruct

    def place(step):
        core = lax.axis_index("c")
        return (1 - core if theirs else core) * 4 + step

    row_block = pl.BlockSpec((ROWS, WIDTH), lambda s: (place(s), 0))
    gain_block = pl.BlockSpec((1, 128), lambda s: (0, place(s)))
    return pl.pallas_call(
        finish_kernel,
        out_shape=[shape((WIDTH, WIDTH), F32), shape((1, WIDTH), F32)],
        grid=(4,),
        in_specs=[pl.BlockSpec((1, 1024, 128), lambda s: (s, 0, 0)), row_block, gain_block]
        + [pl.BlockSpec(memory_space=pl.ANY)] * len(partial),
        out_specs=[row_block, gain_block],
        input_output_aliases={3: 0, 4: 1} if partial else {},
        compiler_params=PARAMS,
        cost_estimate=pl.CostEstimate(flops=1_500_000, bytes_accessed=4_000_000, transcendentals=0),
        name="finish_theirs" if partial else "finish_mine",
    )(source, weight, gain, *partial)


def per_device(query_rows, key_rows, value_rows, gate_rows, lengths, norm_gain, out_weight, cotangent):
    gain = norm_gain.reshape(1, WIDTH)
    swap = [(0, 1), (1, 0)]
    shape = jax.ShapeDtypeStruct
    own = jnp.concatenate([query_rows, key_rows, value_rows, gate_rows, cotangent], axis=0)
    other = lax.ppermute(own, "c", swap)
    part, normed, inv_std, gated_own = pl.pallas_call(
        forward_kernel,
        out_shape=[
            shape((4, 1024, 128), BF16),
            shape((GROUP, WIDTH), F32),
            shape((GROUP, 1), F32),
            shape((ROWS, WIDTH), BF16),
        ],
        in_specs=[SMEM, VMEM, VMEM, VMEM],
        out_specs=[VMEM] * 4,
        scratch_shapes=[pltpu.VMEM((GROUP, WIDTH), F32), pltpu.VMEM((2, GROUP, WIDTH // 2), BF16)],
        compiler_params=PARAMS,
        cost_estimate=pl.CostEstimate(flops=540_000_000, bytes_accessed=6_000_000, transcendentals=300_000),
        name="forward",
    )(lengths, own, other, gain)

    pieces = lax.all_to_all(part, "x", 0, 0, tiled=True)

    layer_out, query_grad, key_grad, value_grad, gate_grad = pl.pallas_call(
        backward_kernel,
        out_shape=[shape((ROWS, WIDTH), BF16)] * 5,
        in_specs=[SMEM] + [VMEM] * 7,
        out_specs=[VMEM] * 5,
        scratch_shapes=[pltpu.VMEM((GROUP, WIDTH), F32), pltpu.VMEM((GROUP, WIDTH), BF16)],
        compiler_params=PARAMS,
        cost_estimate=pl.CostEstimate(flops=1_800_000_000, bytes_accessed=9_000_000, transcendentals=300_000),
        name="backward",
    )(lengths, own, other, gain, normed, inv_std, gated_own, out_weight)

    block = pl.pallas_call(
        chip_sum_kernel,
        out_shape=shape((1024, 128), BF16),
        in_specs=[VMEM],
        out_specs=VMEM,
        compiler_params=PARAMS,
        name="chip_sum",
    )(pieces)
    pieces = lax.all_to_all(block.reshape(64, 16, 128), PLANE, 0, 0, tiled=True)
    total = pl.pallas_call(
        plane_sum_kernel,
        out_shape=shape((64, 16, 128), BF16),
        in_specs=[VMEM],
        out_specs=VMEM,
        compiler_params=PARAMS,
        name="plane_sum",
    )(pieces)
    block = lax.all_to_all(total, PLANE, 0, 0, tiled=True).reshape(1, 1024, 128)
    mine = lax.all_to_all(jnp.broadcast_to(block, (4, 1024, 128)), "x", 0, 0, tiled=True)
    theirs = lax.ppermute(mine, "c", swap)
    partial = finish(False, mine, out_weight, gain, ())
    weight_grad, gain_grad = finish(True, theirs, out_weight, gain, partial)
    return (layer_out, query_grad, key_grad, value_grad, gate_grad, gain_grad.reshape(WIDTH), weight_grad)


def solution(mesh):
    chips = Mesh(mesh.devices.reshape(8, 8, 4, 2), DEVICES)
    rows = P(DEVICES, None)
    return jax.shard_map(
        per_device,
        mesh=chips,
        in_specs=(rows, rows, rows, rows, P(CHIPS, None), P(), P(), rows),
        out_specs=(rows, rows, rows, rows, rows, P(), P()),
        check_vma=False,
    )
```

```python
import functools

import jax
import jax.numpy as jnp
from jax import lax
from jax.experimental import pallas as pl
from jax.experimental.pallas import tpu as pltpu
from jax.sharding import Mesh, PartitionSpec as P

HEADS = 4
HEAD_DIM = 256
WIDTH = 1024
ROWS = 128
GROUP = 256
PLANE = ("z", "y")
CHIPS = ("z", "y", "x")
DEVICES = ("z", "y", "x", "c")
F32 = jnp.float32
BF16 = jnp.bfloat16
VMEM = pl.BlockSpec(memory_space=pltpu.VMEM)
SMEM = pl.BlockSpec(memory_space=pltpu.SMEM)
PARAMS = pltpu.CompilerParams(vmem_limit_bytes=20 * 1024 * 1024)


def dot(a, b, contract):
    return lax.dot_general(a, b, (contract, ((), ())), preferred_element_type=F32)


def visible(lengths, first_row, first_column, size):
    row = first_row + lax.broadcasted_iota(jnp.int32, (size, 1), 0)
    column = first_column + lax.broadcasted_iota(jnp.int32, (size, size), 1)
    start = jnp.zeros((size, 1), jnp.int32)
    end = 0
    for user in range(3):
        end = end + lengths[0, user]
        start = jnp.where(row >= end, end, start)
    return (column <= row) & (column >= start)


QUERY, KEY, VALUE, GATE, COTANGENT = range(5)


def at(core, item):
    first = core * 5 * ROWS + item * ROWS
    return pl.ds(first if isinstance(core, int) else pl.multiple_of(first, ROWS), ROWS)


def both(whole, item, columns):
    return jnp.concatenate([whole[at(0, item), columns], whole[at(1, item), columns]], axis=0)


def head_columns(head):
    return slice(head * HEAD_DIM, (head + 1) * HEAD_DIM)


def gate_rows_of(first, count):
    core, row = divmod(first, ROWS)
    return pl.ds(core * 5 * ROWS + GATE * ROWS + row, count)


def tile(index):
    return slice(index * 16, (index + 1) * 16)


def forward_kernel(lengths, whole, gain, part, normed, inv_std, gated, attended):
    core = lax.axis_index("c")
    mask = visible(lengths, 0, 0, GROUP)
    for head in range(HEADS):
        columns = head_columns(head)
        scores = dot(both(whole, QUERY, columns), both(whole, KEY, columns), ((1,), (1,))) * (HEAD_DIM**-0.5)
        weights = jnp.where(mask, scores * jax.nn.sigmoid(scores), 0.0).astype(BF16)
        attended[:, columns] = dot(weights, both(whole, VALUE, columns), ((1,), (0,)))
    chunk = 32
    for first in range(0, GROUP, chunk):
        rows = slice(first, first + chunk)
        values = attended[rows, :]
        centered = values - jnp.mean(values, axis=1, keepdims=True)
        inverse = lax.rsqrt(jnp.mean(centered * centered, axis=1, keepdims=True) + 1e-05)
        unit = centered * inverse
        normed[rows, :] = unit
        inv_std[rows, :] = inverse
        result = (unit * gain[...] * whole[gate_rows_of(first, chunk), :].astype(F32)).astype(BF16)
        gated[0, rows, :] = result[:, : WIDTH // 2]
        gated[1, rows, :] = result[:, WIDTH // 2 :]
    for x in range(4):
        mine = gated[core, :, x * 128 : (x + 1) * 128]
        for half in range(2):
            wide = slice(half * 512, (half + 1) * 512)
            block = dot(mine, both(whole, COTANGENT, wide), ((0,), (0,))).astype(BF16)
            for i in range(8):
                for j in range(4):
                    part[x, tile(i * 8 + half * 4 + j), :] = block[i * 16 : (i + 1) * 16, j * 128 : (j + 1) * 128]


def finish_rows(theirs, source, weight, gain, weight_grad, gain_grad, rows_out, gain_out, sems):
    core = lax.axis_index("c")
    half = 1 - core if theirs else core
    copies = []
    for x in range(4):
        first = pl.multiple_of(half * 512 + x * ROWS, ROWS)
        total = jnp.zeros((ROWS, 128), F32)
        for j in range(8):
            columns = slice(j * 128, (j + 1) * 128)
            block = jnp.concatenate([source[x, tile(i * 8 + j), :].astype(F32) for i in range(8)], axis=0)
            rows_out[x * ROWS : (x + 1) * ROWS, columns] = block
            total = total + block * weight[pl.ds(first, ROWS), columns].astype(F32)
        copies.append(
            pltpu.make_async_copy(
                rows_out.at[pl.ds(x * ROWS, ROWS), :], weight_grad.at[pl.ds(first, ROWS), :], sems.at[x]
            )
        )
        copies[-1].start()
        gain_out[:, x * 128 : (x + 1) * 128] = jnp.sum(total.T, axis=0, keepdims=True) / gain[:, pl.ds(first, 128)]
    copies.append(pltpu.make_async_copy(gain_out, gain_grad.at[half], sems.at[4]))
    copies[-1].start()
    return copies


def backward_kernel(
    lengths, whole, gain, normed, inv_std, gated, weight, mine,
    layer_hbm, query_hbm, key_hbm, value_hbm, gate_hbm, weight_grad, gain_grad,
    layer_out, query_grad, key_grad, value_grad, gate_grad, gated_grad, out_grad, rows_out, gain_out, sems,
):
    copies = finish_rows(False, mine, weight, gain, weight_grad, gain_grad, rows_out, gain_out, sems)

    def send(source, target, columns=None):
        if columns is not None:
            source, target = source.at[:, columns], target.at[:, columns]
        copies.append(pltpu.make_async_copy(source, target, sems.at[len(copies)]))
        copies[-1].start()

    core = lax.axis_index("c")
    first_own = pl.multiple_of(core * ROWS, ROWS)
    own_rows = pl.ds(first_own, ROWS)
    scale = HEAD_DIM**-0.5
    gated_grad[...] = dot(both(whole, COTANGENT, slice(None)), weight[...], ((1,), (1,)))
    chunk = 16
    for first in range(0, GROUP, chunk):
        rows = slice(first, first + chunk)
        unit = normed[rows, :]
        scaled = gated_grad[rows, :] * gain[...]
        gate_grad[rows, :] = (scaled * unit).astype(BF16)
        inner = scaled * whole[gate_rows_of(first, chunk), :].astype(F32)
        inner = (
            inner
            - jnp.mean(inner, axis=1, keepdims=True)
            - unit * jnp.mean(inner * unit, axis=1, keepdims=True)
        ) * inv_std[rows, :]
        out_grad[rows, :] = inner.astype(BF16)
    send(gate_grad.at[own_rows, :], gate_hbm)
    layer_out[...] = (
        dot(gated[0, own_rows, :], weight[: WIDTH // 2], ((1,), (0,)))
        + dot(gated[1, own_rows, :], weight[WIDTH // 2 :], ((1,), (0,)))
    ).astype(BF16)
    send(layer_out, layer_hbm)
    mask_own, mask_cross = visible(lengths, first_own, first_own, ROWS), visible(lengths, ROWS, 0, ROWS)
    for head in range(HEADS):
        columns = head_columns(head)

        def block(query_core, key_core, grads, mask):
            query, key = whole[at(query_core, QUERY), columns], whole[at(key_core, KEY), columns]
            scores = dot(query, key, ((1,), (1,))) * scale
            sigma = jax.nn.sigmoid(scores)
            weights = jnp.where(mask, scores * sigma, 0.0).astype(BF16)
            slope = sigma * (1.0 + scores * (1.0 - sigma))
            value_dot = dot(grads, whole[at(key_core, VALUE), columns], ((1,), (1,)))
            score_grad = jnp.where(mask, value_dot * slope, 0.0).astype(BF16)
            return (
                dot(score_grad, key, ((1,), (0,))),
                dot(score_grad, query, ((0,), (0,))),
                dot(weights, grads, ((0,), (0,))),
            )

        query_own, key_own, value_own = block(core, core, out_grad[own_rows, columns], mask_own)
        query_cross, key_cross, value_cross = block(1, 0, out_grad[ROWS:, columns], mask_cross)
        query_sum = query_own + jnp.where(core == 1, query_cross, 0.0)
        key_sum = key_own + jnp.where(core == 0, key_cross, 0.0)
        value_sum = value_own + jnp.where(core == 0, value_cross, 0.0)
        query_grad[:, columns] = (query_sum * scale).astype(BF16)
        key_grad[:, columns] = (key_sum * scale).astype(BF16)
        value_grad[:, columns] = value_sum.astype(BF16)
        send(query_grad, query_hbm, columns)
        send(key_grad, key_hbm, columns)
        send(value_grad, value_hbm, columns)
    for copy in copies:
        copy.wait()


def chip_sum_kernel(pieces, total):
    for first in range(0, 1024, 128):
        rows = slice(first, first + 128)
        value = pieces[0, rows, :].astype(F32) + pieces[1, rows, :].astype(F32)
        total[rows, :] = (value + (pieces[2, rows, :].astype(F32) + pieces[3, rows, :].astype(F32))).astype(BF16)


def plane_sum_kernel(pieces, total):
    sums = [pieces[i].astype(F32) for i in range(4)]
    for first in range(4, 64, 4):
        sums = [sums[i] + pieces[first + i].astype(F32) for i in range(4)]
    value = ((sums[0] + sums[1]) + (sums[2] + sums[3])).astype(BF16)
    for i in range(64):
        total[i] = value


def finish_kernel(source, weight, gain, weight_in, gain_in, weight_grad, gain_grad, rows_out, gain_out, sems):
    for copy in finish_rows(True, source, weight, gain, weight_grad, gain_grad, rows_out, gain_out, sems):
        copy.wait()


def per_device(query_rows, key_rows, value_rows, gate_rows, lengths, norm_gain, out_weight, cotangent):
    gain = norm_gain.reshape(1, WIDTH)
    swap = [(0, 1), (1, 0)]
    shape = jax.ShapeDtypeStruct
    own = jnp.concatenate([query_rows, key_rows, value_rows, gate_rows, cotangent], axis=0)
    whole = lax.all_gather(own, "c", axis=0, tiled=True)
    part, normed, inv_std, gated = pl.pallas_call(
        forward_kernel,
        out_shape=[
            shape((4, 1024, 128), BF16),
            shape((GROUP, WIDTH), F32),
            shape((GROUP, 1), F32),
            shape((2, GROUP, WIDTH // 2), BF16),
        ],
        in_specs=[SMEM, VMEM, VMEM],
        out_specs=[VMEM] * 4,
        scratch_shapes=[pltpu.VMEM((GROUP, WIDTH), F32)],
        compiler_params=PARAMS,
        cost_estimate=pl.CostEstimate(flops=540_000_000, bytes_accessed=6_000_000, transcendentals=300_000),
        name="forward",
    )(lengths, whole, gain)

    pieces = lax.all_to_all(part, "x", 0, 0, tiled=True)

    block = pl.pallas_call(
        chip_sum_kernel,
        out_shape=shape((1024, 128), BF16),
        in_specs=[VMEM],
        out_specs=VMEM,
        compiler_params=PARAMS,
        name="chip_sum",
    )(pieces)
    pieces = lax.all_to_all(block.reshape(64, 16, 128), PLANE, 0, 0, tiled=True)
    total = pl.pallas_call(
        plane_sum_kernel,
        out_shape=shape((64, 16, 128), BF16),
        in_specs=[VMEM],
        out_specs=VMEM,
        compiler_params=PARAMS,
        name="plane_sum",
    )(pieces)
    block = lax.all_to_all(total, PLANE, 0, 0, tiled=True).reshape(1, 1024, 128)
    mine = lax.all_to_all(jnp.broadcast_to(block, (4, 1024, 128)), "x", 0, 0, tiled=True)
    theirs = lax.ppermute(mine, "c", swap)
    anywhere = pl.BlockSpec(memory_space=pl.ANY)
    sums = [shape((WIDTH, WIDTH), F32), shape((2, 1, WIDTH // 2), F32)]
    staging = [pltpu.VMEM((WIDTH // 2, WIDTH), F32), pltpu.VMEM((1, WIDTH // 2), F32)]
    *grads, weight_part, gain_part = pl.pallas_call(
        backward_kernel,
        out_shape=[shape((ROWS, WIDTH), BF16)] * 5 + sums,
        in_specs=[SMEM] + [VMEM] * 7,
        out_specs=[anywhere] * 7,
        scratch_shapes=[pltpu.VMEM((ROWS, WIDTH), BF16)] * 4
        + [pltpu.VMEM((GROUP, WIDTH), BF16)]
        + [pltpu.VMEM((GROUP, WIDTH), F32), pltpu.VMEM((GROUP, WIDTH), BF16)]
        + staging
        + [pltpu.SemaphoreType.DMA((19,))],
        compiler_params=PARAMS,
        cost_estimate=pl.CostEstimate(flops=1_800_000_000, bytes_accessed=9_000_000, transcendentals=300_000),
        name="backward",
    )(lengths, whole, gain, normed, inv_std, gated, out_weight, mine)
    weight_grad, gain_grad = pl.pallas_call(
        finish_kernel,
        out_shape=sums,
        in_specs=[VMEM] * 3 + [anywhere] * 2,
        out_specs=[anywhere] * 2,
        input_output_aliases={3: 0, 4: 1},
        scratch_shapes=staging + [pltpu.SemaphoreType.DMA((5,))],
        compiler_params=PARAMS,
        cost_estimate=pl.CostEstimate(flops=1_500_000, bytes_accessed=4_000_000, transcendentals=0),
        name="finish",
    )(theirs, out_weight, gain, weight_part, gain_part)
    return (*grads, gain_grad.reshape(WIDTH), weight_grad)


def solution(mesh):
    chips = Mesh(mesh.devices.reshape(8, 8, 4, 2), DEVICES)
    rows = P(DEVICES, None)
    return jax.shard_map(
        per_device,
        mesh=chips,
        in_specs=(rows, rows, rows, rows, P(CHIPS, None), P(), P(), rows),
        out_specs=(rows, rows, rows, rows, rows, P(), P()),
        check_vma=False,
    )
```

```python
import functools

import jax
import jax.numpy as jnp
from jax import lax
from jax.experimental import pallas as pl
from jax.experimental.pallas import tpu as pltpu
from jax.sharding import Mesh, PartitionSpec as P

HEADS = 4
HEAD_DIM = 256
WIDTH = 1024
ROWS = 128
GROUP = 256
PLANE = ("z", "y")
CHIPS = ("z", "y", "x")
DEVICES = ("z", "y", "x", "c")
F32 = jnp.float32
BF16 = jnp.bfloat16
VMEM = pl.BlockSpec(memory_space=pltpu.VMEM)
SMEM = pl.BlockSpec(memory_space=pltpu.SMEM)
PARAMS = pltpu.CompilerParams(vmem_limit_bytes=20 * 1024 * 1024)


def dot(a, b, contract):
    return lax.dot_general(a, b, (contract, ((), ())), preferred_element_type=F32)


def visible_mask(core, lengths):
    def place(shape, axis):
        local = lax.broadcasted_iota(jnp.int32, shape, axis)
        return jnp.where(local < ROWS, core * ROWS + local, (1 - core) * ROWS + local - ROWS)

    row, column = place((GROUP, 1), 0), place((GROUP, GROUP), 1)
    start = jnp.zeros((GROUP, 1), jnp.int32)
    end = 0
    for user in range(3):
        end = end + lengths[0, user]
        start = jnp.where(row >= end, end, start)
    return (column <= row) & (column >= start)


def both(own, other, item, columns):
    rows = slice(item * ROWS, (item + 1) * ROWS)
    return jnp.concatenate([own[rows, columns], other[rows, columns]], axis=0)


def head_columns(head):
    return slice(head * HEAD_DIM, (head + 1) * HEAD_DIM)


def tile(index):
    return slice(index * 16, (index + 1) * 16)


def forward_kernel(lengths, own, other, gain, part, normed, inv_std, gated_own, attended, gated):
    core = lax.axis_index("c")
    visible = visible_mask(core, lengths)
    for head in range(HEADS):
        columns = head_columns(head)
        scores = dot(both(own, other, 0, columns), both(own, other, 1, columns), ((1,), (1,))) * (HEAD_DIM**-0.5)
        weights = jnp.where(visible, scores * jax.nn.sigmoid(scores), 0.0).astype(BF16)
        attended[:, columns] = dot(weights, both(own, other, 2, columns), ((1,), (0,)))
    chunk = 32
    for first in range(0, GROUP, chunk):
        rows = slice(first, first + chunk)
        values = attended[rows, :]
        centered = values - jnp.mean(values, axis=1, keepdims=True)
        inverse = lax.rsqrt(jnp.mean(centered * centered, axis=1, keepdims=True) + 1e-05)
        unit = centered * inverse
        normed[rows, :] = unit
        inv_std[rows, :] = inverse
        source, at = (own, first) if first < ROWS else (other, first - ROWS)
        gate = source[3 * ROWS + at : 3 * ROWS + at + chunk, :].astype(F32)
        result = (unit * gain[...] * gate).astype(BF16)
        gated[0, rows, :] = result[:, : WIDTH // 2]
        gated[1, rows, :] = result[:, WIDTH // 2 :]
        if first < ROWS:
            gated_own[rows, :] = result
    for x in range(4):
        mine = gated[core, :, x * 128 : (x + 1) * 128]
        for half in range(2):
            wide = slice(half * 512, (half + 1) * 512)
            block = dot(mine, both(own, other, 4, wide), ((0,), (0,))).astype(BF16)
            for i in range(8):
                for j in range(4):
                    part[x, tile(i * 8 + half * 4 + j), :] = block[i * 16 : (i + 1) * 16, j * 128 : (j + 1) * 128]


def finish_rows(theirs, source, weight, gain, weight_grad, gain_grad, rows_out, gain_out, sems):
    core = lax.axis_index("c")
    half = 1 - core if theirs else core
    copies = []
    for x in range(4):
        first = pl.multiple_of(half * 512 + x * ROWS, ROWS)
        total = jnp.zeros((ROWS, 128), F32)
        for j in range(8):
            columns = slice(j * 128, (j + 1) * 128)
            block = jnp.concatenate([source[x, tile(i * 8 + j), :].astype(F32) for i in range(8)], axis=0)
            rows_out[x * ROWS : (x + 1) * ROWS, columns] = block
            total = total + block * weight[pl.ds(first, ROWS), columns].astype(F32)
        copies.append(
            pltpu.make_async_copy(
                rows_out.at[pl.ds(x * ROWS, ROWS), :], weight_grad.at[pl.ds(first, ROWS), :], sems.at[x]
            )
        )
        copies[-1].start()
        gain_out[:, x * 128 : (x + 1) * 128] = jnp.sum(total.T, axis=0, keepdims=True) / gain[:, pl.ds(first, 128)]
    copies.append(pltpu.make_async_copy(gain_out, gain_grad.at[half], sems.at[4]))
    copies[-1].start()
    return copies


def backward_kernel(
    lengths, own, other, gain, normed, inv_std, gated_own, weight, mine,
    layer_hbm, query_hbm, key_hbm, value_hbm, gate_hbm, weight_grad, gain_grad,
    layer_out, query_grad, key_grad, value_grad, gate_grad, gated_grad, out_grad, rows_out, gain_out, sems,
):
    copies = finish_rows(False, mine, weight, gain, weight_grad, gain_grad, rows_out, gain_out, sems)

    def send(source, target, columns=None):
        if columns is not None:
            source, target = source.at[:, columns], target.at[:, columns]
        copies.append(pltpu.make_async_copy(source, target, sems.at[len(copies)]))
        copies[-1].start()

    scale = HEAD_DIM**-0.5
    gated_grad[...] = dot(both(own, other, 4, slice(None)), weight[...], ((1,), (1,)))
    chunk = 16
    for first in range(0, GROUP, chunk):
        rows = slice(first, first + chunk)
        unit = normed[rows, :]
        source, at = (own, first) if first < ROWS else (other, first - ROWS)
        gate = source[3 * ROWS + at : 3 * ROWS + at + chunk, :].astype(F32)
        scaled = gated_grad[rows, :] * gain[...]
        if first < ROWS:
            gate_grad[rows, :] = (scaled * unit).astype(BF16)
        inner = scaled * gate
        inner = (
            inner
            - jnp.mean(inner, axis=1, keepdims=True)
            - unit * jnp.mean(inner * unit, axis=1, keepdims=True)
        ) * inv_std[rows, :]
        out_grad[rows, :] = inner.astype(BF16)
    send(gate_grad, gate_hbm)
    layer_out[...] = dot(gated_own[...], weight[...], ((1,), (0,))).astype(BF16)
    send(layer_out, layer_hbm)
    visible = visible_mask(lax.axis_index("c"), lengths)
    for head in range(HEADS):
        columns = head_columns(head)
        queries, keys = both(own, other, 0, columns), both(own, other, 1, columns)
        values, grads = both(own, other, 2, columns), out_grad[:, columns]
        scores = dot(queries, keys, ((1,), (1,))) * scale
        sigma = jax.nn.sigmoid(scores)
        weights = jnp.where(visible, scores * sigma, 0.0).astype(BF16)
        slope = sigma * (1.0 + scores * (1.0 - sigma))
        score_grad = jnp.where(visible, dot(grads, values, ((1,), (1,))) * slope, 0.0).astype(BF16)
        query_grad[:, columns] = (dot(score_grad[:ROWS, :], keys, ((1,), (0,))) * scale).astype(BF16)
        key_grad[:, columns] = (dot(score_grad[:, :ROWS], queries, ((0,), (0,))) * scale).astype(BF16)
        value_grad[:, columns] = dot(weights[:, :ROWS], grads, ((0,), (0,))).astype(BF16)
        send(query_grad, query_hbm, columns)
        send(key_grad, key_hbm, columns)
        send(value_grad, value_hbm, columns)
    for copy in copies:
        copy.wait()


def chip_sum_kernel(pieces, total):
    for first in range(0, 1024, 128):
        rows = slice(first, first + 128)
        value = pieces[0, rows, :].astype(F32) + pieces[1, rows, :].astype(F32)
        total[rows, :] = (value + (pieces[2, rows, :].astype(F32) + pieces[3, rows, :].astype(F32))).astype(BF16)


def plane_sum_kernel(pieces, total):
    sums = [pieces[i].astype(F32) for i in range(4)]
    for first in range(4, 64, 4):
        sums = [sums[i] + pieces[first + i].astype(F32) for i in range(4)]
    value = ((sums[0] + sums[1]) + (sums[2] + sums[3])).astype(BF16)
    for i in range(64):
        total[i] = value


def finish_kernel(source, weight, gain, weight_in, gain_in, weight_grad, gain_grad, rows_out, gain_out, sems):
    for copy in finish_rows(True, source, weight, gain, weight_grad, gain_grad, rows_out, gain_out, sems):
        copy.wait()


def per_device(query_rows, key_rows, value_rows, gate_rows, lengths, norm_gain, out_weight, cotangent):
    gain = norm_gain.reshape(1, WIDTH)
    swap = [(0, 1), (1, 0)]
    shape = jax.ShapeDtypeStruct
    own = jnp.concatenate([query_rows, key_rows, value_rows, gate_rows, cotangent], axis=0)
    other = lax.ppermute(own, "c", swap)
    part, normed, inv_std, gated_own = pl.pallas_call(
        forward_kernel,
        out_shape=[
            shape((4, 1024, 128), BF16),
            shape((GROUP, WIDTH), F32),
            shape((GROUP, 1), F32),
            shape((ROWS, WIDTH), BF16),
        ],
        in_specs=[SMEM, VMEM, VMEM, VMEM],
        out_specs=[VMEM] * 4,
        scratch_shapes=[pltpu.VMEM((GROUP, WIDTH), F32), pltpu.VMEM((2, GROUP, WIDTH // 2), BF16)],
        compiler_params=PARAMS,
        cost_estimate=pl.CostEstimate(flops=540_000_000, bytes_accessed=6_000_000, transcendentals=300_000),
        name="forward",
    )(lengths, own, other, gain)

    pieces = lax.all_to_all(part, "x", 0, 0, tiled=True)

    block = pl.pallas_call(
        chip_sum_kernel,
        out_shape=shape((1024, 128), BF16),
        in_specs=[VMEM],
        out_specs=VMEM,
        compiler_params=PARAMS,
        name="chip_sum",
    )(pieces)
    pieces = lax.all_to_all(block.reshape(64, 16, 128), PLANE, 0, 0, tiled=True)
    total = pl.pallas_call(
        plane_sum_kernel,
        out_shape=shape((64, 16, 128), BF16),
        in_specs=[VMEM],
        out_specs=VMEM,
        compiler_params=PARAMS,
        name="plane_sum",
    )(pieces)
    block = lax.all_to_all(total, PLANE, 0, 0, tiled=True).reshape(1, 1024, 128)
    mine = lax.all_to_all(jnp.broadcast_to(block, (4, 1024, 128)), "x", 0, 0, tiled=True)
    theirs = lax.ppermute(mine, "c", swap)
    anywhere = pl.BlockSpec(memory_space=pl.ANY)
    sums = [shape((WIDTH, WIDTH), F32), shape((2, 1, WIDTH // 2), F32)]
    staging = [pltpu.VMEM((WIDTH // 2, WIDTH), F32), pltpu.VMEM((1, WIDTH // 2), F32)]
    *grads, weight_part, gain_part = pl.pallas_call(
        backward_kernel,
        out_shape=[shape((ROWS, WIDTH), BF16)] * 5 + sums,
        in_specs=[SMEM] + [VMEM] * 8,
        out_specs=[anywhere] * 7,
        scratch_shapes=[pltpu.VMEM((ROWS, WIDTH), BF16)] * 5
        + [pltpu.VMEM((GROUP, WIDTH), F32), pltpu.VMEM((GROUP, WIDTH), BF16)]
        + staging
        + [pltpu.SemaphoreType.DMA((19,))],
        compiler_params=PARAMS,
        cost_estimate=pl.CostEstimate(flops=1_800_000_000, bytes_accessed=9_000_000, transcendentals=300_000),
        name="backward",
    )(lengths, own, other, gain, normed, inv_std, gated_own, out_weight, mine)
    weight_grad, gain_grad = pl.pallas_call(
        finish_kernel,
        out_shape=sums,
        in_specs=[VMEM] * 3 + [anywhere] * 2,
        out_specs=[anywhere] * 2,
        input_output_aliases={3: 0, 4: 1},
        scratch_shapes=staging + [pltpu.SemaphoreType.DMA((5,))],
        compiler_params=PARAMS,
        cost_estimate=pl.CostEstimate(flops=1_500_000, bytes_accessed=4_000_000, transcendentals=0),
        name="finish",
    )(theirs, out_weight, gain, weight_part, gain_part)
    return (*grads, gain_grad.reshape(WIDTH), weight_grad)


def solution(mesh):
    chips = Mesh(mesh.devices.reshape(8, 8, 4, 2), DEVICES)
    rows = P(DEVICES, None)
    return jax.shard_map(
        per_device,
        mesh=chips,
        in_specs=(rows, rows, rows, rows, P(CHIPS, None), P(), P(), rows),
        out_specs=(rows, rows, rows, rows, rows, P(), P()),
        check_vma=False,
    )
```

```python
import functools

import jax
import jax.numpy as jnp
from jax import lax
from jax.experimental import pallas as pl
from jax.experimental.pallas import tpu as pltpu
from jax.sharding import Mesh, PartitionSpec as P

HEADS = 4
HEAD_DIM = 256
WIDTH = 1024
ROWS = 128
GROUP = 256
PLANE = ("y", "z")
CHIPS = ("z", "y", "x")
DEVICES = ("z", "y", "x", "c")
F32 = jnp.float32
BF16 = jnp.bfloat16
VMEM = pl.BlockSpec(memory_space=pltpu.VMEM)
SMEM = pl.BlockSpec(memory_space=pltpu.SMEM)
PARAMS = pltpu.CompilerParams(vmem_limit_bytes=20 * 1024 * 1024)


def dot(a, b, contract):
    return lax.dot_general(a, b, (contract, ((), ())), preferred_element_type=F32)


def visible_mask(core, lengths):
    def place(shape, axis):
        local = lax.broadcasted_iota(jnp.int32, shape, axis)
        return jnp.where(local < ROWS, core * ROWS + local, (1 - core) * ROWS + local - ROWS)

    row, column = place((GROUP, 1), 0), place((GROUP, GROUP), 1)
    start = jnp.zeros((GROUP, 1), jnp.int32)
    end = 0
    for user in range(3):
        end = end + lengths[0, user]
        start = jnp.where(row >= end, end, start)
    return (column <= row) & (column >= start)


def both(own, other, item, columns):
    rows = slice(item * ROWS, (item + 1) * ROWS)
    return jnp.concatenate([own[rows, columns], other[rows, columns]], axis=0)


def head_columns(head):
    return slice(head * HEAD_DIM, (head + 1) * HEAD_DIM)


def tile(index):
    return slice(index * 16, (index + 1) * 16)


def forward_kernel(lengths, own, other, gain, part, normed, inv_std, gated_own, attended, gated):
    core = lax.axis_index("c")
    visible = visible_mask(core, lengths)
    for head in range(HEADS):
        columns = head_columns(head)
        scores = dot(both(own, other, 0, columns), both(own, other, 1, columns), ((1,), (1,))) * (HEAD_DIM**-0.5)
        weights = jnp.where(visible, scores * jax.nn.sigmoid(scores), 0.0).astype(BF16)
        attended[:, columns] = dot(weights, both(own, other, 2, columns), ((1,), (0,)))
    chunk = 32
    for first in range(0, GROUP, chunk):
        rows = slice(first, first + chunk)
        values = attended[rows, :]
        centered = values - jnp.mean(values, axis=1, keepdims=True)
        inverse = lax.rsqrt(jnp.mean(centered * centered, axis=1, keepdims=True) + 1e-05)
        unit = centered * inverse
        normed[rows, :] = unit
        inv_std[rows, :] = inverse
        source, at = (own, first) if first < ROWS else (other, first - ROWS)
        gate = source[3 * ROWS + at : 3 * ROWS + at + chunk, :].astype(F32)
        result = (unit * gain[...] * gate).astype(BF16)
        gated[0, rows, :] = result[:, : WIDTH // 2]
        gated[1, rows, :] = result[:, WIDTH // 2 :]
        if first < ROWS:
            gated_own[rows, :] = result
    for x in range(4):
        mine = gated[core, :, x * 128 : (x + 1) * 128]
        for half in range(2):
            wide = slice(half * 512, (half + 1) * 512)
            block = dot(mine, both(own, other, 4, wide), ((0,), (0,))).astype(BF16)
            for i in range(8):
                for j in range(4):
                    part[x, tile(i * 8 + half * 4 + j), :] = block[i * 16 : (i + 1) * 16, j * 128 : (j + 1) * 128]


def finish_rows(theirs, source, weight, gain, weight_grad, gain_grad, rows_out, gain_out, sems):
    core = lax.axis_index("c")
    half = 1 - core if theirs else core
    copies = []
    for x in range(4):
        first = pl.multiple_of(half * 512 + x * ROWS, ROWS)
        total = jnp.zeros((ROWS, 128), F32)
        for j in range(8):
            columns = slice(j * 128, (j + 1) * 128)
            block = jnp.concatenate([source[x, tile(i * 8 + j), :].astype(F32) for i in range(8)], axis=0)
            rows_out[x * ROWS : (x + 1) * ROWS, columns] = block
            total = total + block * weight[pl.ds(first, ROWS), columns].astype(F32)
        copies.append(
            pltpu.make_async_copy(
                rows_out.at[pl.ds(x * ROWS, ROWS), :], weight_grad.at[pl.ds(first, ROWS), :], sems.at[x]
            )
        )
        copies[-1].start()
        gain_out[:, x * 128 : (x + 1) * 128] = jnp.sum(total.T, axis=0, keepdims=True) / gain[:, pl.ds(first, 128)]
    copies.append(pltpu.make_async_copy(gain_out, gain_grad.at[half], sems.at[4]))
    copies[-1].start()
    return copies


def backward_kernel(
    lengths, own, other, gain, normed, inv_std, gated_own, weight, mine,
    layer_hbm, query_hbm, key_hbm, value_hbm, gate_hbm, weight_grad, gain_grad,
    layer_out, query_grad, key_grad, value_grad, gate_grad, gated_grad, out_grad, rows_out, gain_out, sems,
):
    copies = finish_rows(False, mine, weight, gain, weight_grad, gain_grad, rows_out, gain_out, sems)

    def send(source, target, columns=None):
        if columns is not None:
            source, target = source.at[:, columns], target.at[:, columns]
        copies.append(pltpu.make_async_copy(source, target, sems.at[len(copies)]))
        copies[-1].start()

    scale = HEAD_DIM**-0.5
    gated_grad[...] = dot(both(own, other, 4, slice(None)), weight[...], ((1,), (1,)))
    chunk = 16
    for first in range(0, GROUP, chunk):
        rows = slice(first, first + chunk)
        unit = normed[rows, :]
        source, at = (own, first) if first < ROWS else (other, first - ROWS)
        gate = source[3 * ROWS + at : 3 * ROWS + at + chunk, :].astype(F32)
        scaled = gated_grad[rows, :] * gain[...]
        if first < ROWS:
            gate_grad[rows, :] = (scaled * unit).astype(BF16)
        inner = scaled * gate
        inner = (
            inner
            - jnp.mean(inner, axis=1, keepdims=True)
            - unit * jnp.mean(inner * unit, axis=1, keepdims=True)
        ) * inv_std[rows, :]
        out_grad[rows, :] = inner.astype(BF16)
    send(gate_grad, gate_hbm)
    layer_out[...] = dot(gated_own[...], weight[...], ((1,), (0,))).astype(BF16)
    send(layer_out, layer_hbm)
    visible = visible_mask(lax.axis_index("c"), lengths)
    for head in range(HEADS):
        columns = head_columns(head)
        queries, keys = both(own, other, 0, columns), both(own, other, 1, columns)
        values, grads = both(own, other, 2, columns), out_grad[:, columns]
        scores = dot(queries, keys, ((1,), (1,))) * scale
        sigma = jax.nn.sigmoid(scores)
        weights = jnp.where(visible, scores * sigma, 0.0).astype(BF16)
        slope = sigma * (1.0 + scores * (1.0 - sigma))
        score_grad = jnp.where(visible, dot(grads, values, ((1,), (1,))) * slope, 0.0).astype(BF16)
        query_grad[:, columns] = (dot(score_grad[:ROWS, :], keys, ((1,), (0,))) * scale).astype(BF16)
        key_grad[:, columns] = (dot(score_grad[:, :ROWS], queries, ((0,), (0,))) * scale).astype(BF16)
        value_grad[:, columns] = dot(weights[:, :ROWS], grads, ((0,), (0,))).astype(BF16)
        send(query_grad, query_hbm, columns)
        send(key_grad, key_hbm, columns)
        send(value_grad, value_hbm, columns)
    for copy in copies:
        copy.wait()


def chip_sum_kernel(pieces, total):
    for first in range(0, 1024, 128):
        rows = slice(first, first + 128)
        value = pieces[0, rows, :].astype(F32) + pieces[1, rows, :].astype(F32)
        total[rows, :] = (value + (pieces[2, rows, :].astype(F32) + pieces[3, rows, :].astype(F32))).astype(BF16)


def plane_sum_kernel(pieces, total):
    sums = [pieces[i].astype(F32) for i in range(4)]
    for first in range(4, 64, 4):
        sums = [sums[i] + pieces[first + i].astype(F32) for i in range(4)]
    value = ((sums[0] + sums[1]) + (sums[2] + sums[3])).astype(BF16)
    for i in range(64):
        total[i] = value


def finish_kernel(source, weight, gain, weight_in, gain_in, weight_grad, gain_grad, rows_out, gain_out, sems):
    for copy in finish_rows(True, source, weight, gain, weight_grad, gain_grad, rows_out, gain_out, sems):
        copy.wait()


def per_device(query_rows, key_rows, value_rows, gate_rows, lengths, norm_gain, out_weight, cotangent):
    gain = norm_gain.reshape(1, WIDTH)
    swap = [(0, 1), (1, 0)]
    shape = jax.ShapeDtypeStruct
    own = jnp.concatenate([query_rows, key_rows, value_rows, gate_rows, cotangent], axis=0)
    other = lax.ppermute(own, "c", swap)
    part, normed, inv_std, gated_own = pl.pallas_call(
        forward_kernel,
        out_shape=[
            shape((4, 1024, 128), BF16),
            shape((GROUP, WIDTH), F32),
            shape((GROUP, 1), F32),
            shape((ROWS, WIDTH), BF16),
        ],
        in_specs=[SMEM, VMEM, VMEM, VMEM],
        out_specs=[VMEM] * 4,
        scratch_shapes=[pltpu.VMEM((GROUP, WIDTH), F32), pltpu.VMEM((2, GROUP, WIDTH // 2), BF16)],
        compiler_params=PARAMS,
        cost_estimate=pl.CostEstimate(flops=540_000_000, bytes_accessed=6_000_000, transcendentals=300_000),
        name="forward",
    )(lengths, own, other, gain)

    pieces = lax.all_to_all(part, "x", 0, 0, tiled=True)

    block = pl.pallas_call(
        chip_sum_kernel,
        out_shape=shape((1024, 128), BF16),
        in_specs=[VMEM],
        out_specs=VMEM,
        compiler_params=PARAMS,
        name="chip_sum",
    )(pieces)
    pieces = lax.all_to_all(block.reshape(64, 16, 128), PLANE, 0, 0, tiled=True)
    total = pl.pallas_call(
        plane_sum_kernel,
        out_shape=shape((64, 16, 128), BF16),
        in_specs=[VMEM],
        out_specs=VMEM,
        compiler_params=PARAMS,
        name="plane_sum",
    )(pieces)
    block = lax.all_to_all(total, PLANE, 0, 0, tiled=True).reshape(1, 1024, 128)
    mine = lax.all_to_all(jnp.broadcast_to(block, (4, 1024, 128)), "x", 0, 0, tiled=True)
    theirs = lax.ppermute(mine, "c", swap)
    anywhere = pl.BlockSpec(memory_space=pl.ANY)
    sums = [shape((WIDTH, WIDTH), F32), shape((2, 1, WIDTH // 2), F32)]
    staging = [pltpu.VMEM((WIDTH // 2, WIDTH), F32), pltpu.VMEM((1, WIDTH // 2), F32)]
    *grads, weight_part, gain_part = pl.pallas_call(
        backward_kernel,
        out_shape=[shape((ROWS, WIDTH), BF16)] * 5 + sums,
        in_specs=[SMEM] + [VMEM] * 8,
        out_specs=[anywhere] * 7,
        scratch_shapes=[pltpu.VMEM((ROWS, WIDTH), BF16)] * 5
        + [pltpu.VMEM((GROUP, WIDTH), F32), pltpu.VMEM((GROUP, WIDTH), BF16)]
        + staging
        + [pltpu.SemaphoreType.DMA((19,))],
        compiler_params=PARAMS,
        cost_estimate=pl.CostEstimate(flops=1_800_000_000, bytes_accessed=9_000_000, transcendentals=300_000),
        name="backward",
    )(lengths, own, other, gain, normed, inv_std, gated_own, out_weight, mine)
    weight_grad, gain_grad = pl.pallas_call(
        finish_kernel,
        out_shape=sums,
        in_specs=[VMEM] * 3 + [anywhere] * 2,
        out_specs=[anywhere] * 2,
        input_output_aliases={3: 0, 4: 1},
        scratch_shapes=staging + [pltpu.SemaphoreType.DMA((5,))],
        compiler_params=PARAMS,
        cost_estimate=pl.CostEstimate(flops=1_500_000, bytes_accessed=4_000_000, transcendentals=0),
        name="finish",
    )(theirs, out_weight, gain, weight_part, gain_part)
    return (*grads, gain_grad.reshape(WIDTH), weight_grad)


def solution(mesh):
    chips = Mesh(mesh.devices.reshape(8, 8, 4, 2), DEVICES)
    rows = P(DEVICES, None)
    return jax.shard_map(
        per_device,
        mesh=chips,
        in_specs=(rows, rows, rows, rows, P(CHIPS, None), P(), P(), rows),
        out_specs=(rows, rows, rows, rows, rows, P(), P()),
        check_vma=False,
    )
```
